32 devices in a mesh: crop: 2 (over y), row: 4 (over x, core), col: 4 (over z).
Axes of the slice: x: 2, y: 2, z: 4, core: 2. Of those that a mesh axis runs over, the one named last changes fastest.
Arguments:
- pair: bfloat16 [1536, 768, 128], P(('crop', 'col'), 'row'), parts along dimension 0, may hold values from -40 to 40
- chain_ids: int32 [1536], P('crop'), parts along dimension 0, may hold values from 0 to 3, never falling along the last dimension, each value on 1 to 384 neighbouring positions
- block_keep: int32 [12, 6], P('crop'), parts along dimension 0, may hold values 0 or 1
- norm_gain: float32 [128], replicated, may hold values from 0.1 to 1.9
- norm_bias: float32 [128], replicated, may hold values from -3 to 3
- left_weight: bfloat16 [128, 256], replicated, may hold values from -0.5 to 0.5
- right_weight: bfloat16 [128, 256], replicated, may hold values from -0.5 to 0.5
- gate_weight: bfloat16 [128, 128], replicated, may hold values from -0.5 to 0.5
- out_gain: float32 [128], replicated, may hold values from 0.1 to 1.9
- out_bias: float32 [128], replicated, may hold values from -3 to 3
- out_weight: bfloat16 [128, 128], replicated, may hold values from -0.5 to 0.5
Outputs:
- update: bfloat16 [1536, 768, 128], P(('crop', 'col'), 'row'), parts along dimension 0
The draws below stay inside these ranges and needn't reach their ends.
There are 2 independent parts, one for each index of `crop`. The reference program is written for one: setup_inputs(seed, part) draws one part's arguments, and reference() takes and returns one part's arrays. A program takes and returns all parts, laid end to end along the dimension named above; an argument that names none is the same for every part. Nothing has to cross between parts.
Inputs may be any that keep to these rules, and one draw needn't show every extreme that they name: `chain_ids`: chain ids never fall along the crop; every one of the 4 chains holds 1 to 384 tokens, one of them exactly that many.
All inputs are finite; a program needn't handle non-finite values.
Results may differ from the reference program's by a relative error of at most 0.0095.
Values may be sent and summed in bfloat16 or wider, within the bound.
A program may use at most 448 MiB of HBM per device.

```python
import math
import jax
import jax.numpy as jnp
import numpy as np
from jax import lax

C = 128
H = 128
N = 768
BLOCK = 128
CHAINS = 4
NB = 6
KSHARD = 192


def draw_pair(key, part):
    key = jax.random.fold_in(key, 11)
    cell_key, chan_key, base_key = jax.random.split(key, 3)
    cell_scale = jnp.exp(jax.random.uniform(cell_key, (N, N, 1), jnp.float32, 0.0, 2.3))
    chan_scale = jnp.exp(jax.random.uniform(chan_key, (1, 1, C), jnp.float32, 0.0, 2.3))
    base = jax.random.normal(base_key, (N, N, C), jnp.float32)
    return (jnp.clip(base, -4.0, 4.0) * cell_scale * chan_scale * 0.1).astype(jnp.bfloat16)


def place_ends(values, own_key, low, largest):
    shape = values.shape
    index_at = [jax.random.randint(jax.random.fold_in(own_key, axis), (), 0, shape[axis]) for axis in range(len(shape))]
    values = values.at[tuple(index_at)].set(low)
    longest = shape.index(max(shape))
    index_at[longest] = (index_at[longest] + 1) % shape[longest]
    return values.at[tuple(index_at)].set(largest)


def length_profile(count, total, most, skew):
    weights = [(1 << 20) // math.isqrt(rank ** skew) + 1 for rank in range(2, count + 1)]
    surplus, counts = total - most - (count - 1), [1] * (count - 1)
    while surplus > 0:
        candidates = [i for i in range(count - 1) if counts[i] < most]
        whole, budget = sum([weights[i] for i in candidates]), surplus
        for i in candidates:
            extra = min(most - counts[i], max(1, budget * weights[i] // whole), surplus)
            counts[i] = counts[i] + extra
            surplus = surplus - extra
    return np.array([most] + counts)


def uneven_parts(stream_key, number_of, total, bound, lean):
    if number_of == 2:
        one = jax.random.randint(stream_key, (), max(1, total - bound), min(bound, total - 1) + 1)
        return jnp.stack([one, total - one])
    tallies = jnp.asarray(length_profile(number_of, total, bound, lean), jnp.int32)
    twos = (number_of - 1) // 2
    giver, receiver = tallies[1:1 + 2 * twos:2], tallies[2:2 + 2 * twos:2]
    slack = jnp.minimum(giver - 1, bound - receiver)
    shifted = jax.random.randint(jax.random.fold_in(stream_key, 1), (twos,), 0, 1 << 20) % (slack + 1)
    tallies = tallies.at[1:1 + 2 * twos:2].set(giver - shifted).at[2:2 + 2 * twos:2].set(receiver + shifted)
    return tallies[jax.random.permutation(jax.random.fold_in(stream_key, 2), number_of)]


def normal_values(rng, extent, scale, reach, kind=jnp.bfloat16):
    array = scale * jax.random.normal(rng, extent, jnp.float32)
    return jnp.clip(array, min=-reach, max=reach).astype(kind)


def setup_inputs(seed: int = 0, part: int = 0) -> dict:
    key_list = jax.random.split(jax.random.key(seed), 12)
    part_keys = jax.random.split(jax.random.fold_in(key_list[11], part), 12)
    pair = draw_pair(jax.random.fold_in(jax.random.fold_in(key_list[11], part), 71), part)
    chain_ids = jnp.searchsorted(jnp.cumsum(uneven_parts(part_keys[1], CHAINS, N, N // 2, 0)), jnp.arange(N), side="right").astype(jnp.int32)
    block_keep = place_ends((jax.random.randint(part_keys[2], (NB, NB), 0, 4) < 1).astype(jnp.int32), jax.random.fold_in(part_keys[2], 1), 0, 1)
    norm_gain = jnp.clip(1.0 + 0.18 * jax.random.normal(key_list[3], (C,), jnp.float32), 0.1, 1.9)
    norm_bias = normal_values(key_list[4], (C,), 0.5, 3.0, jnp.float32)
    left_weight = normal_values(key_list[5], (C, 2 * H), C ** -0.5, 0.5)
    right_weight = normal_values(key_list[6], (C, 2 * H), C ** -0.5, 0.5)
    gate_weight = normal_values(key_list[7], (C, C), C ** -0.5, 0.5)
    out_gain = jnp.clip(1.0 + 0.18 * jax.random.normal(key_list[8], (H,), jnp.float32), 0.1, 1.9)
    out_bias = normal_values(key_list[9], (H,), 0.5, 3.0, jnp.float32)
    out_weight = normal_values(key_list[10], (H, C), H ** -0.5, 0.5)
    return {"pair": pair, "chain_ids": chain_ids, "block_keep": block_keep, "norm_gain": norm_gain, "norm_bias": norm_bias, "left_weight": left_weight, "right_weight": right_weight, "gate_weight": gate_weight, "out_gain": out_gain, "out_bias": out_bias, "out_weight": out_weight}


def layer_norm(values, gain, bias):
    mean = lax.optimization_barrier(jnp.mean(values, axis=-1, keepdims=True))
    centered = values - mean
    spread = lax.optimization_barrier(jnp.mean(centered * centered, axis=-1, keepdims=True))
    return centered * lax.rsqrt(spread + 1e-05) * gain + bias

def gated_projection(normed, weight, mask):
    hidden = weight.shape[1] // 2
    both = jnp.dot(normed.reshape(-1, normed.shape[-1]), weight, preferred_element_type=jnp.float32)
    both = both.reshape(normed.shape[:-1] + (2 * hidden,))
    return (mask[..., None] * jax.nn.sigmoid(both[..., hidden:]) * both[..., :hidden]).astype(jnp.bfloat16)

def reference(pair, chain_ids, block_keep, norm_gain, norm_bias, left_weight, right_weight, gate_weight, out_gain, out_bias, out_weight):
    normed = layer_norm(pair.astype(jnp.float32), norm_gain, norm_bias).astype(jnp.bfloat16)
    blocks = (jnp.arange(N, dtype=jnp.int32) // BLOCK).astype(jnp.int32)
    kept = block_keep[blocks][:, blocks].astype(jnp.float32)
    same = chain_ids[:, None] == chain_ids[None, :]
    mask = jnp.where(same, jnp.ones_like(kept), kept)
    left = gated_projection(normed, left_weight, mask)
    right = gated_projection(normed, right_weight, mask)

    def add_group(step, total):
        start = (step * KSHARD).astype(jnp.int32)
        left_part = lax.dynamic_slice_in_dim(left, start, KSHARD, 1).astype(jnp.float32)
        right_part = lax.dynamic_slice_in_dim(right, start, KSHARD, 1).astype(jnp.float32)
        partial_sum = jnp.einsum('ikh,jkh->ijh', left_part, right_part)
        rounded = lax.optimization_barrier(partial_sum.astype(jnp.bfloat16))
        return total + rounded.astype(jnp.float32)
    summed = lax.fori_loop(0, N // KSHARD, add_group, jnp.zeros((N, N, H), jnp.float32))
    out_normed = layer_norm(summed, out_gain, out_bias).astype(jnp.bfloat16)
    gate = jax.nn.sigmoid(jnp.dot(normed.reshape(-1, C), gate_weight, preferred_element_type=jnp.float32))
    projected = jnp.dot(out_normed.reshape(-1, H), out_weight, preferred_element_type=jnp.float32)
    return (gate * projected).reshape(N, N, C).astype(jnp.bfloat16)
```

```python
import jax
import jax.numpy as jnp
from jax import lax
from jax.sharding import PartitionSpec as P

BLOCK = 128


def layer_norm(values, gain, bias):
    mean = jnp.mean(values, axis=-1, keepdims=True)
    centered = values - mean
    spread = jnp.mean(centered * centered, axis=-1, keepdims=True)
    return centered * lax.rsqrt(spread + 1e-05) * gain + bias


def gated_projection(normed, weight, mask):
    hidden = weight.shape[1] // 2
    both = jnp.dot(normed.reshape(-1, normed.shape[-1]), weight, preferred_element_type=jnp.float32)
    both = both.reshape(normed.shape[:-1] + (2 * hidden,))
    return (mask[..., None] * jax.nn.sigmoid(both[..., hidden:]) * both[..., :hidden]).astype(
        jnp.bfloat16
    )


def block_table(start, count, blocks):
    positions = start + lax.iota(jnp.int32, count)
    return ((positions // BLOCK)[:, None] == lax.iota(jnp.int32, blocks)[None, :]).astype(
        jnp.float32
    )


def pair_mask(chain_ids, keep_table, row_start, row_count, col_start, col_count):
    row_chain = lax.dynamic_slice_in_dim(chain_ids, row_start, row_count)
    col_chain = lax.dynamic_slice_in_dim(chain_ids, col_start, col_count)
    blocks = keep_table.shape[0]
    left_table = block_table(row_start, row_count, blocks)
    right_table = block_table(col_start, col_count, blocks)
    kept = jnp.dot(jnp.dot(left_table, keep_table), right_table.T)
    return jnp.where(row_chain[:, None] == col_chain[None, :], jnp.ones_like(kept), kept)


def shards(
    pair,
    chain_ids,
    block_keep,
    norm_gain,
    norm_bias,
    left_weight,
    right_weight,
    gate_weight,
    out_gain,
    out_bias,
    out_weight,
):
    tile_rows, tile_cols, channels = pair.shape
    hidden = left_weight.shape[1] // 2
    row_start = lax.axis_index("col") * tile_rows
    col_start = lax.axis_index("row") * tile_cols
    keep_table = block_keep.astype(jnp.float32)
    normed = layer_norm(pair.astype(jnp.float32), norm_gain, norm_bias).astype(jnp.bfloat16)
    local_mask = pair_mask(chain_ids, keep_table, row_start, tile_rows, col_start, tile_cols)
    left = gated_projection(normed, left_weight, local_mask)
    piece = lax.all_gather(normed, "col", axis=0, tiled=True)
    piece_mask = pair_mask(
        chain_ids, keep_table, jnp.int32(0), piece.shape[0], col_start, tile_cols
    )
    right_all = gated_projection(piece, right_weight, piece_mask)
    summed = lax.psum_scatter(
        jnp.einsum("jkh,ikh->jih", right_all, left, preferred_element_type=jnp.float32).astype(
            jnp.bfloat16
        ),
        "row",
        scatter_dimension=0,
        tiled=True,
    ).astype(jnp.float32)
    out_normed = jnp.swapaxes(layer_norm(summed, out_gain, out_bias).astype(jnp.bfloat16), 0, 1)
    gate = jax.nn.sigmoid(
        jnp.dot(normed.reshape(-1, channels), gate_weight, preferred_element_type=jnp.float32)
    )
    projected = jnp.dot(
        out_normed.reshape(-1, hidden), out_weight, preferred_element_type=jnp.float32
    )
    return (gate * projected).reshape(tile_rows, tile_cols, channels).astype(jnp.bfloat16)


NEIGHBOUR = ((0, 1), (1, 0), (2, 3), (3, 2))
MIDDLE = ((1, 2), (2, 1))
CORE_PAIRS = ((0, 1), (1, 0), (2, 3), (3, 2))
CHIP_PAIRS = ((0, 2), (2, 0), (1, 3), (3, 1))
FIRST_BLOCK = (0, 2, 1, 3)
SECOND_BLOCK = (1, 3, 0, 2)
OTHER_BLOCK = (1, 0, 3, 2)
CHUNKS = 4


def pick(table, index):
    result = jnp.int32(table[0])
    for position in range(1, len(table)):
        result = jnp.where(index == position, jnp.int32(table[position]), result)
    return result


def owners():
    moves = []
    for layer in range(4):
        for slot in range(4):
            i_block = (layer, OTHER_BLOCK[layer])[slot // 2]
            j_block = (FIRST_BLOCK[layer], SECOND_BLOCK[layer])[slot % 2]
            moves.append((slot * 4 + layer, j_block * 4 + i_block))
    return tuple(move for move in moves if move[0] != move[1])


def sum_over_row(partial, place):
    core, chip = place % 2, place // 2
    kept = lax.dynamic_index_in_dim(partial, core, 1, keepdims=False)
    sent = lax.dynamic_index_in_dim(partial, 1 - core, 1, keepdims=False)
    came = lax.ppermute(sent, "row", CORE_PAIRS)
    pairs = (kept.astype(jnp.float32) + came.astype(jnp.float32)).astype(jnp.bfloat16)
    kept = lax.dynamic_index_in_dim(pairs, chip, 0, keepdims=False)
    sent = lax.dynamic_index_in_dim(pairs, 1 - chip, 0, keepdims=False)
    came = lax.ppermute(sent, "row", CHIP_PAIRS)
    return (kept.astype(jnp.float32) + came.astype(jnp.float32)).astype(jnp.bfloat16)


def blocked(
    pair,
    chain_ids,
    block_keep,
    norm_gain,
    norm_bias,
    left_weight,
    right_weight,
    gate_weight,
    out_gain,
    out_bias,
    out_weight,
):
    tile_rows, tile_cols, channels = pair.shape
    hidden = left_weight.shape[1] // 2
    depth = tile_rows // CHUNKS
    layer = lax.axis_index("col")
    place = lax.axis_index("row")
    col_start = place * tile_cols
    keep_table = block_keep.astype(jnp.float32)
    at_end = (layer == 0) | (layer == 3)
    stays = jnp.bool_(False)
    moved_from = [move[0] for move in owners()]
    for spot in range(16):
        if spot not in moved_from:
            stays = stays | (place * 4 + layer == spot)

    def mask_of(block, chunk):
        start = block * tile_rows + chunk * depth
        return pair_mask(chain_ids, keep_table, start, depth, col_start, tile_cols)

    own, other, first, second = [], [], [], []
    for chunk in range(CHUNKS):
        piece = pair[chunk * depth : (chunk + 1) * depth]
        own.append(layer_norm(piece.astype(jnp.float32), norm_gain, norm_bias).astype(jnp.bfloat16))
        other.append(lax.ppermute(own[chunk], "col", NEIGHBOUR))
        first.append(jnp.where(at_end, own[chunk], lax.ppermute(own[chunk], "col", MIDDLE)))
        second.append(jnp.where(at_end, other[chunk], lax.ppermute(other[chunk], "col", MIDDLE)))

    left = []
    for block, pieces in ((layer, own), (pick(OTHER_BLOCK, layer), other)):
        parts = [
            gated_projection(pieces[chunk], left_weight, mask_of(block, chunk))
            for chunk in range(CHUNKS)
        ]
        left.append(jnp.concatenate(parts, axis=0))
    left = jnp.stack(left)

    gate_in = jnp.concatenate(own, axis=0)
    results = []
    for chunk in range(CHUNKS):
        right = jnp.stack(
            [
                gated_projection(
                    pieces[chunk], right_weight, mask_of(pick(table, layer), chunk)
                )
                for table, pieces in ((FIRST_BLOCK, first), (SECOND_BLOCK, second))
            ]
        )
        partial = jnp.einsum(
            "pjkh,qikh->qpjih", right, left, preferred_element_type=jnp.float32
        ).astype(jnp.bfloat16)
        summed = sum_over_row(partial, place)
        moved = lax.ppermute(summed, ("row", "col"), owners())
        summed = jnp.where(stays, summed, moved).astype(jnp.float32)
        out_normed = jnp.swapaxes(
            layer_norm(summed, out_gain, out_bias).astype(jnp.bfloat16), 0, 1
        )
        gate = jax.nn.sigmoid(
            jnp.dot(
                gate_in[:, chunk * depth : (chunk + 1) * depth].reshape(-1, channels),
                gate_weight,
                preferred_element_type=jnp.float32,
            )
        )
        projected = jnp.dot(
            out_normed.reshape(-1, hidden), out_weight, preferred_element_type=jnp.float32
        )
        results.append(
            (gate * projected).reshape(tile_rows, depth, channels).astype(jnp.bfloat16)
        )
    return jnp.concatenate(results, axis=1)


def solution(mesh):
    placed = (
        P(("crop", "col"), "row", None),
        P("crop"),
        P("crop", None),
        P(),
        P(),
        P(),
        P(),
        P(),
        P(),
        P(),
        P(),
    )
    return jax.shard_map(
        blocked if (mesh.shape["col"], mesh.shape["row"]) == (4, 4) else shards,
        mesh=mesh,
        in_specs=placed,
        out_specs=P(("crop", "col"), "row", None),
        check_vma=False,
    )
```
